32 devices in a mesh: grp: 2 (over y), slab: 4 (over z), ang: 2 (over x), rep: 2 (over core).
Axes of the slice: x: 2, y: 2, z: 4, core: 2. Of those that a mesh axis runs over, the one named last changes fastest.
Arguments:
- volume: float32 [64, 512], P(('grp', 'slab'), 'rep'), parts along dimension 0, may hold values from 0.5 to 2
- measured: float32 [32, 8, 2048], P(('grp', 'ang'), None, 'slab'), parts along dimension 0, may hold values from 0.5 to 8
- in_plane: bfloat16 [16, 4, 512, 2048], P('ang', 'slab', 'rep'), may hold values from 0.0009994507 to 0.0099487305
- pair_bands: int32 [16, 4, 5], P('ang', 'slab'), may hold values from 0 to 3, as said below
- pair_counts: int32 [16, 4], P('ang', 'slab'), may hold values from 2 to 4, as said below
- pair_weight_tiles: float32 [16, 4, 5, 2, 8], P('ang', 'slab'), may hold values from 0.01 to 0.1
Outputs:
- new_volume: float32 [64, 512], P(('grp', 'slab'), 'rep'), parts along dimension 0
- residual: float32 [32, 8, 2048], P(('grp', 'ang'), ('slab', 'rep')), parts along dimension 0
The draws below stay inside these ranges and needn't reach their ends.
There are 2 independent parts, one for each index of `grp`. The reference program is written for one: setup_inputs(seed, part) draws one part's arguments, and reference() takes and returns one part's arrays. A program takes and returns all parts, laid end to end along the dimension named above; an argument that names none is the same for every part. Nothing has to cross between parts.
Inputs may be any that keep to these rules, and one draw needn't show every extreme that they name: `pair_bands`: for angle a and slab s the first pair_counts[a, s] entries are the consecutive bands from max(0, s - h) to min(3, s + h) in increasing order, for some h of 1 to 2; the other entries are 0. Every band is listed by its own slab. `pair_counts`: the length of each list as described for pair_bands.
All inputs are finite; a program needn't handle non-finite values.
Results may differ from the reference program's by a relative error of at most 0.0003.
Values may be sent and summed in bfloat16 or wider, within the bound.
A program may use at most 64 MiB of HBM per device.

```python
import math
import jax
import jax.numpy as jnp
from jax import lax

NA = 16
U = 2048
XY = 512
ZS = 8
RPD = 2
SLABS = 4
SPAN = 2
CAP = 5
NV = 8
NZ = 32


def band_spans(key):
    reach_of = jax.random.randint(jax.random.fold_in(key, 11), (NA, SLABS), 1, SPAN + 1)
    middle = jax.random.randint(jax.random.fold_in(key, 12), (NA,), 1, SLABS - SPAN)
    slab_ids = jnp.arange(SLABS, dtype=jnp.int32)
    reach_of = jnp.where(slab_ids[None, :] == 1, SPAN, reach_of)
    reach_of = jnp.where(slab_ids[None, :] == middle[:, None], SPAN, reach_of)
    reach_of = jnp.where(slab_ids[None, :] == 0, 1, reach_of)
    first_band = jnp.maximum(slab_ids[None, :] - reach_of, 0)
    last_band = jnp.minimum(slab_ids[None, :] + reach_of, SLABS - 1)
    counts = last_band - first_band + 1
    slot_ids = jnp.arange(CAP, dtype=jnp.int32)
    listed = jnp.where(slot_ids[None, None, :] < counts[:, :, None], first_band[:, :, None] + slot_ids[None, None, :], 0)
    return (listed.astype(jnp.int32), counts.astype(jnp.int32))


def draw_pair_bands(key, part):
    listed, counts = band_spans(key)
    return listed


def draw_pair_counts(key, part):
    listed, counts = band_spans(key)
    return counts


def block_levels(own_key, shape, shards, least, largest):
    gain, own = 1.0, jax.random.fold_in(own_key, 6)
    for dim, shards_of in shards:
        steps = jnp.exp(jax.random.uniform(jax.random.fold_in(own, dim), (shards_of,), jnp.float32, least / len(shards), largest / len(shards)))
        gain = gain * jnp.repeat(steps, shape[dim] // shards_of).reshape([-1 if axis == dim else 1 for axis in range(len(shape))])
    return gain


def setup_inputs(seed: int = 0, part: int = 0) -> dict:
    splits = jax.random.split(jax.random.key(seed), 7)
    part_splits = jax.random.split(jax.random.fold_in(splits[6], part), 7)
    volume = jnp.clip(0.5 + 1.5 * jax.random.uniform(part_splits[0], (NZ, XY), jnp.float32) ** block_levels(part_splits[0], (NZ, XY), ((0, 4), (1, 2)), -0.2, 0.2), 0.5, 2.0)
    measured = jnp.clip(0.5 + 7.5 * jax.random.uniform(part_splits[1], (NA, NV, U), jnp.float32) ** block_levels(part_splits[1], (NA, NV, U), ((0, 2), (2, 4)), -0.2, 0.2), 0.5, 8.0)
    in_plane = jnp.clip(jnp.exp(math.log(0.0099487305) - 2.2979944 * jax.random.uniform(splits[2], (NA, SLABS, XY, U), jnp.float32) ** block_levels(splits[2], (NA, SLABS, XY, U), ((0, 2), (1, 4), (2, 2)), -0.2, 0.2)), 0.0009994507, 0.0099487305).astype(jnp.bfloat16)
    pair_bands = draw_pair_bands(jax.random.fold_in(splits[6], 71), part)
    pair_counts = draw_pair_counts(jax.random.fold_in(splits[6], 71), part)
    pair_weight_tiles = jnp.clip(jnp.exp(math.log(0.1) - 2.3025851 * jax.random.uniform(splits[5], (NA, SLABS, CAP, RPD, ZS), jnp.float32) ** block_levels(splits[5], (NA, SLABS, CAP, RPD, ZS), ((0, 2), (1, 4)), -0.2, 0.2)), 0.01, 0.1)
    return dict(volume=volume, measured=measured, in_plane=in_plane, pair_bands=pair_bands, pair_counts=pair_counts, pair_weight_tiles=pair_weight_tiles)


def reference(volume, measured, in_plane, pair_bands, pair_counts, pair_weight_tiles):
    largest_index = lax.Precision.HIGHEST
    rounded = lax.optimization_barrier(volume.astype(jnp.bfloat16))
    stacked = rounded.astype(jnp.float32).reshape(SLABS, ZS, XY)

    def per_angle(footprint):
        widened = footprint.astype(jnp.float32)
        projected = jnp.einsum('szx,sxu->szu', stacked, widened, precision=largest_index)
        return projected, jnp.sum(widened, axis=1), jnp.sum(widened, axis=2)

    plane_proj, plane_ones, voxel_rays = lax.map(per_angle, in_plane)
    slot_ids = jnp.arange(CAP, dtype=jnp.int32)
    active_slot = slot_ids[None, None, :] < pair_counts[:, :, None]
    band_ids = jnp.arange(SLABS, dtype=jnp.int32)
    picked_blocks = (pair_bands[:, :, :, None] == band_ids[None, None, None, :]) & active_slot[:, :, :, None]
    tile_lookup = jnp.einsum('vmht,vmhyn->vmtyn', picked_blocks.astype(jnp.float32), pair_weight_tiles, precision=largest_index)
    forward = jnp.einsum('asdrz,aszu->adru', tile_lookup, plane_proj, precision=largest_index).reshape(NA, NV, U)
    ray_sums = jnp.einsum('asdr,asu->adru', jnp.sum(tile_lookup, axis=4), plane_ones, precision=largest_index).reshape(NA, NV, U)
    residual = (measured - forward) / ray_sums
    residual_b = lax.optimization_barrier(residual.astype(jnp.bfloat16)).astype(jnp.float32)
    back_rows = jnp.einsum('asdrz,adru->aszu', tile_lookup, residual_b.reshape(NA, SLABS, RPD, U), precision=largest_index)
    back_b = lax.optimization_barrier(back_rows.astype(jnp.bfloat16))

    def add_angle(total, items):
        rows_b, footprint = items
        term = jnp.einsum('szu,sxu->szx', rows_b.astype(jnp.float32), footprint.astype(jnp.float32), precision=largest_index)
        return total + term, None

    update, ignored = lax.scan(add_angle, jnp.zeros((SLABS, ZS, XY), jnp.float32), (back_b, in_plane))
    voxel_sums = jnp.einsum('asz,asx->szx', jnp.sum(tile_lookup, axis=(2, 3)), voxel_rays, precision=largest_index)
    new_volume = volume + (update / voxel_sums).reshape(NZ, XY)
    return new_volume, residual
```

```python
import functools

import jax
import jax.numpy as jnp
from jax import lax
from jax.experimental import pallas as pl
from jax.experimental.pallas import tpu as pltpu
from jax.sharding import PartitionSpec as P

MESH = pl.DeviceIdType.MESH
F32 = jnp.float32
BF16 = jnp.bfloat16
EXACT = lax.Precision.HIGHEST
LANES = 128
ROWS = 8
WEIGHT_MAX = 0.0099487305
VOLUME_MAX = 2.0
HALF_CODE = 32500.0
CHUNKS = 4


def each(count, fn):
    if count <= 8:
        for i in range(count):
            fn(i)
    else:
        pl.loop(0, count)(fn)


def kernel(
    cfg,
    volume, measured, in_plane, bands, counts, tiles,
    new_volume, residual,
    wide, rows_t, bd_raw, bd_mean, tw, proj,
    meas_send, meas_recv, half_own, half_send, half_recv,
    code_send, code_recv, gather, res_all, res_wide, acc, x_send, x_recv,
    w_sem, ms_s, ms_r, f_s, f_r, q_s, q_r, r_s, r_r, p_s, p_r, x_s, x_r,
):
    slabs, angs, span, angles, zs, cw, chunks, strip = cfg
    me = lax.axis_index("slab")
    rep = lax.axis_index("rep")
    ang = lax.axis_index("ang")
    other = 1 - rep
    nrow = slabs * ROWS
    nz = angles * zs
    xy = volume.shape[1]
    xy_all = 2 * xy
    mean_scale = 2 * HALF_CODE / (xy_all * VOLUME_MAX * WEIGHT_MAX * 1.001)
    ones_scale = 2 * HALF_CODE / (xy_all * WEIGHT_MAX * 1.001)

    def cols(k):
        return pl.ds(k * cw, cw)

    def block(d):
        return pl.ds(pl.multiple_of(d * ROWS, ROWS), ROWS)

    def load(k):
        return pltpu.make_async_copy(in_plane.at[:, 0, :, cols(k)], wide.at[k], w_sem.at[k])

    def remote(src, dst, s, r, to):
        return pltpu.make_async_remote_copy(
            src_ref=src, dst_ref=dst, send_sem=s, recv_sem=r, device_id=to, device_id_type=MESH
        )

    def meas_copy(d, slot):
        return remote(meas_send.at[d], meas_recv.at[slot], ms_s.at[d], ms_r.at[slot], {"slab": d})

    def half_copy(k):
        return remote(half_send.at[k], half_recv.at[k], f_s.at[k], f_r.at[k], {"rep": other})

    def code_copy(k, d, slot):
        return remote(code_send.at[k, d], code_recv.at[k, slot], q_s.at[k, d], q_r.at[k, slot], {"slab": d})

    def res_copy(k, d, slot):
        src = gather.at[k, 0, me]
        return remote(src, gather.at[k, 0, slot], r_s.at[k, d], r_r.at[k, slot], {"slab": d})

    def pass_copy(k, s):
        return remote(gather.at[k, 0, s], gather.at[k, 1, s], p_s.at[k, s], p_r.at[k, s], {"rep": other})

    def x_copy(to, slot):
        return remote(x_send, x_recv.at[slot], x_s.at[to], x_r.at[slot], {"ang": to})

    def near(fn):
        def one(i):
            d = me + (span - i // 2) * (1 - 2 * (i % 2))

            @pl.when((d >= 0) & (d < slabs))
            def _():
                fn(d)

        each(2 * span, one)

    def others(count, mine, fn):
        each(count - 1, lambda i: fn(lax.rem(mine + i + 1, count)))

    for k in range(chunks):
        load(k).start()

    if angles < ROWS:
        meas_send[...] = jnp.zeros_like(meas_send)
        half_own[...] = jnp.zeros_like(half_own)
        half_send[...] = jnp.zeros_like(half_send)
    rows_t[...] = jnp.zeros_like(rows_t)
    gather[...] = jnp.zeros_like(gather)

    barrier = pltpu.get_barrier_semaphore()
    others(slabs, me, lambda d: pl.semaphore_signal(barrier, inc=1, device_id={"slab": d}, device_id_type=MESH))
    others(angs, ang, lambda d: pl.semaphore_signal(barrier, inc=1, device_id={"ang": d}, device_id_type=MESH))
    pl.semaphore_signal(barrier, inc=1, device_id={"rep": other}, device_id_type=MESH)

    def fill(d):
        for a in range(angles):
            meas_send[d, a : a + 1, LANES : LANES + strip] = measured[a, pl.ds(d * 2 + rep, 1), :]
            first = bands[a, 0, 0]
            count = counts[a, 0]
            listed = jnp.where((d >= first) & (d < first + count), F32(1), F32(0))
            slot = jnp.clip(d - first, 0, tiles.shape[2] - 1)
            rows_t[0, d, a : a + 1, 0:zs] = tiles[a, 0, slot, pl.ds(rep, 1), :] * listed
            rows_t[1, d, a : a + 1, 0:zs] = tiles[a, 0, slot, pl.ds(other, 1), :] * listed

    each(slabs, fill)

    lane = lax.broadcasted_iota(jnp.int32, (ROWS, LANES), 1)
    row = lax.broadcasted_iota(jnp.int32, (ROWS, LANES), 0)
    same = (lane // zs) == row

    def blocks(d):
        for r in range(2):
            y = rows_t[r, d]
            weight = jnp.sum(y, axis=1, keepdims=True)
            if r == 0:
                meas_send[d, :, 0:LANES] = jnp.broadcast_to(weight, (ROWS, LANES))
            width = zs
            while width < nz:
                y = y + pltpu.roll(y, width, 1)
                width *= 2
            y = jnp.where(same, y, 0.0)[:, :nz]
            at = block(r * slabs + d)
            bd_raw[at, :] = y
            bd_mean[at, :] = y * (mean_scale / jnp.maximum(weight, 1e-30))

    each(slabs, blocks)
    pl.semaphore_wait(barrier, slabs + angs - 1)
    others(slabs, me, lambda d: meas_copy(d, me).start())

    tw[...] = lax.dot_general(
        bd_raw[...], jnp.ones((2 * nrow, LANES), F32), (((0,), (0,)), ((), ())),
        precision=EXACT, preferred_element_type=F32,
    )
    acc[...] = jnp.zeros_like(acc)
    left = jnp.concatenate([volume[...], jnp.ones_like(volume)], axis=0).astype(BF16)

    def project(k):
        load(k).wait()
        for a in range(angles):
            got = jnp.dot(left, wide[k, a], preferred_element_type=F32)
            proj[a * zs : (a + 1) * zs, :] = got[0:zs]
            half_own[k, nrow + a : nrow + a + 1, :] = got[zs : zs + 1]
            half_send[k, nrow + a : nrow + a + 1, :] = got[zs : zs + 1]
        mix = jnp.dot(bd_mean[...], proj[...], precision=EXACT, preferred_element_type=F32)
        half_own[k, 0:nrow, :] = mix[0:nrow]
        half_send[k, 0:nrow, :] = mix[nrow:]
        half_copy(k).start()

    def scatter(k):
        half_copy(k).wait_recv()
        ones = half_own[k, nrow:, :] + half_recv[k, nrow:, :]
        ones_code = jnp.round(ones * ones_scale - HALF_CODE)

        def send(d):
            mean = half_own[k, block(d), :] + half_recv[k, block(d), :]
            code = jnp.concatenate([jnp.round(mean - HALF_CODE), ones_code], axis=0)
            code_send[k, d] = code.astype(jnp.int32).astype(jnp.int16)
            code_copy(k, d, me).start()

        near(send)

    def wide_weight(s):
        return jnp.concatenate([meas_recv[s, :, 0:LANES]] * (cw // LANES), axis=1)

    def own_weight():
        return jnp.concatenate([meas_send[me, :, 0:LANES]] * (cw // LANES), axis=1)

    def solve(k):
        if k == 0:
            others(slabs, me, lambda s: meas_copy(s, s).wait_recv())
            meas_recv[me] = meas_send[me]
        weight = own_weight()
        res_wide[0:ROWS, :] = weight * (half_own[k, block(me), :] + half_recv[k, block(me), :])
        res_wide[ROWS:, :] = weight * ((half_own[k, nrow:, :] + half_recv[k, nrow:, :]) * ones_scale)

        def add(s):
            code_copy(k, s, s).wait_recv()
            code = code_recv[k, s].astype(jnp.int32).astype(F32) + HALF_CODE
            weight = wide_weight(s)
            res_wide[0:ROWS, :] += weight * code[0:ROWS]
            res_wide[ROWS:, :] += weight * code[ROWS:]

        near(add)
        if strip <= cw:
            each_k = cw // strip
            row_meas = jnp.concatenate(
                [meas_recv[k * each_k + j, :, LANES : LANES + strip] for j in range(each_k)], axis=1
            )
        else:
            start = (k * cw) % strip
            row_meas = meas_recv[(k * cw) // strip, :, LANES + start : LANES + start + cw]
        res = (row_meas - res_wide[0:ROWS, :] * (1.0 / mean_scale)) / (res_wide[ROWS:, :] * (1.0 / ones_scale))
        if angles < ROWS:
            res = jnp.where(lax.broadcasted_iota(jnp.int32, res.shape, 0) < angles, res, 0.0)
        residual[:, cols(k)] = res[0:angles]
        gather[k, 0, me] = jnp.concatenate([res[:, : cw // 2], res[:, cw // 2 :]], axis=0).astype(BF16)
        near(lambda d: res_copy(k, d, me).start())
        pass_copy(k, me).start()

    def relay(k):
        def one(s):
            res_copy(k, s, s).wait_recv()
            pass_copy(k, s).start()

        near(one)

    def back(k):
        near(lambda s: pass_copy(k, s).wait_recv())
        pass_copy(k, me).wait_recv()
        for r in range(2):

            def spread(d):
                got = gather[k, r, d].astype(F32)
                at = block(r * slabs + d)
                res_all[at, : cw // 2] = got[0:ROWS]
                res_all[at, cw // 2 :] = got[ROWS:]

            each(slabs, spread)
        rows_back = lax.dot_general(
            bd_raw[...], res_all[...], (((0,), (0,)), ((), ())), precision=EXACT, preferred_element_type=F32
        )
        update = acc[0:zs, :]
        sums = acc[zs:, :]
        ones = jnp.ones((zs, cw), F32)
        for a in range(angles):
            lhs = jnp.concatenate([rows_back[a * zs : (a + 1) * zs], ones], axis=0).astype(BF16)
            got = lax.dot_general(lhs, wide[k, a], (((1,), (1,)), ((), ())), preferred_element_type=F32)
            update = update + got[0:zs]
            weight = jnp.concatenate([tw[a * zs : (a + 1) * zs, :]] * (xy // LANES), axis=1)
            sums = sums + weight * got[zs:]
        acc[0:zs, :] = update
        acc[zs:, :] = sums

    stages = (project, scatter, solve, relay, back)
    lags = (0, 1, 2, 3, 4)
    for step in range(chunks + lags[-1]):
        for stage, lag in zip(stages, lags):
            if 0 <= step - lag < chunks:
                stage(step - lag)

    x_send[...] = acc[...]
    others(angs, ang, lambda to: x_copy(to, ang).start())
    others(angs, ang, lambda s: x_copy(s, s).wait_recv())
    x_recv[ang] = x_send[...]
    total = x_recv[0]
    for i in range(1, angs):
        total = total + x_recv[i]
    new_volume[...] = volume[...] + total[0:zs] / total[zs:]

    others(slabs, me, lambda d: meas_copy(d, me).wait_send())
    others(angs, ang, lambda to: x_copy(to, ang).wait_send())
    for k in range(chunks):
        half_copy(k).wait_send()
        pass_copy(k, me).wait_send()

        def done(d):
            code_copy(k, d, me).wait_send()
            res_copy(k, d, me).wait_send()
            pass_copy(k, d).wait_send()

        near(done)


def body(mesh, volume, measured, in_plane, pair_bands, pair_counts, pair_weight_tiles):
    slabs, angs = mesh.shape["slab"], mesh.shape["ang"]
    angles, _, xy, width = in_plane.shape
    zs = volume.shape[0]
    span = (pair_weight_tiles.shape[2] - 1) // 2
    chunks = CHUNKS
    cw = width // chunks
    strip = measured.shape[2]
    cfg = (slabs, angs, span, angles, zs, cw, chunks, strip)
    nrow, nz = slabs * ROWS, angles * zs
    dma = pltpu.SemaphoreType.DMA
    vmem = pl.BlockSpec(memory_space=pltpu.VMEM)
    smem = pl.BlockSpec(memory_space=pltpu.SMEM)
    new_volume, residual = pl.pallas_call(
        functools.partial(kernel, cfg),
        out_shape=(
            jax.ShapeDtypeStruct((zs, xy), F32),
            jax.ShapeDtypeStruct((angles, width), F32),
        ),
        in_specs=[vmem, vmem, pl.BlockSpec(memory_space=pl.ANY), smem, smem, vmem],
        out_specs=(vmem, vmem),
        scratch_shapes=[
            pltpu.VMEM((chunks, angles, xy, cw), BF16),
            pltpu.VMEM((2, slabs, ROWS, LANES), F32),
            pltpu.VMEM((2 * nrow, nz), F32),
            pltpu.VMEM((2 * nrow, nz), F32),
            pltpu.VMEM((nz, LANES), F32),
            pltpu.VMEM((nz, cw), F32),
            pltpu.VMEM((slabs, ROWS, LANES + strip), F32),
            pltpu.VMEM((slabs, ROWS, LANES + strip), F32),
            pltpu.VMEM((chunks, nrow + ROWS, cw), F32),
            pltpu.VMEM((chunks, nrow + ROWS, cw), F32),
            pltpu.VMEM((chunks, nrow + ROWS, cw), F32),
            pltpu.VMEM((chunks, slabs, 2 * ROWS, cw), jnp.int16),
            pltpu.VMEM((chunks, slabs, 2 * ROWS, cw), jnp.int16),
            pltpu.VMEM((chunks, 2, slabs, 2 * ROWS, cw // 2), BF16),
            pltpu.VMEM((2 * nrow, cw), F32),
            pltpu.VMEM((2 * ROWS, cw), F32),
            pltpu.VMEM((2 * zs, xy), F32),
            pltpu.VMEM((2 * zs, xy), F32),
            pltpu.VMEM((angs, 2 * zs, xy), F32),
            dma((chunks,)),
            dma((slabs,)), dma((slabs,)),
            dma((chunks,)), dma((chunks,)),
            dma((chunks, slabs)), dma((chunks, slabs)),
            dma((chunks, slabs)), dma((chunks, slabs)),
            dma((chunks, slabs)), dma((chunks, slabs)),
            dma((angs,)), dma((angs,)),
        ],
        compiler_params=pltpu.CompilerParams(
            collective_id=0, has_side_effects=True, vmem_limit_bytes=40 * 1024 * 1024
        ),
        cost_estimate=pl.CostEstimate(
            flops=8 * angles * zs * xy * width, bytes_accessed=2 * angles * xy * width, transcendentals=0
        ),
    )(volume, measured, in_plane, pair_bands, pair_counts, pair_weight_tiles)
    return new_volume, residual.reshape(angles, 1, width)


def solution(mesh):
    return jax.shard_map(
        functools.partial(body, mesh),
        mesh=mesh,
        in_specs=(
            P(("grp", "slab"), "rep"),
            P(("grp", "ang"), None, "slab"),
            P("ang", "slab", "rep", None),
            P("ang", "slab", None),
            P("ang", "slab"),
            P("ang", "slab", None, None, None),
        ),
        out_specs=(P(("grp", "slab"), "rep"), P(("grp", "ang"), ("slab", "rep"), None)),
        check_vma=False,
    )
```

```python
import functools

import jax
import jax.numpy as jnp
from jax import lax
from jax.experimental import pallas as pl
from jax.experimental.pallas import tpu as pltpu
from jax.sharding import PartitionSpec as P

MESH = pl.DeviceIdType.MESH
F32 = jnp.float32
BF16 = jnp.bfloat16
EXACT = lax.Precision.HIGHEST
LANES = 128
ROWS = 8
WEIGHT_MAX = 0.0099487305
VOLUME_MAX = 2.0
HALF_CODE = 32500.0
CHUNKS = 2


def each(count, fn):
    if count <= 8:
        for i in range(count):
            fn(i)
    else:
        pl.loop(0, count)(fn)


def kernel(
    cfg,
    volume_in, measured_in, in_plane, bands_in, counts_in, tiles_in,
    new_volume, residual,
    volume, measured, bands, counts, tiles,
    wide, rows_t, bd_raw, bd_mean, tw, proj,
    meas_send, meas_recv, half_own, half_send, half_recv,
    code_send, code_recv, gather, res_all, res_wide, acc, x_send, x_recv,
    in_sem, w_sem, ms_s, ms_r, f_s, f_r, q_s, q_r, r_s, r_r, p_s, p_r, x_s, x_r,
):
    slabs, angs, span, angles, zs, cw, chunks, strip = cfg
    me = lax.axis_index("slab")
    rep = lax.axis_index("rep")
    ang = lax.axis_index("ang")
    other = 1 - rep
    nrow = slabs * ROWS
    nz = angles * zs
    xy = volume.shape[1]
    xy_all = 2 * xy
    mean_scale = 2 * HALF_CODE / (xy_all * VOLUME_MAX * WEIGHT_MAX * 1.001)
    ones_scale = 2 * HALF_CODE / (xy_all * WEIGHT_MAX * 1.001)

    def cols(k):
        return pl.ds(k * cw, cw)

    def block(d):
        return pl.ds(pl.multiple_of(d * ROWS, ROWS), ROWS)

    def load(k):
        return pltpu.make_async_copy(in_plane.at[:, 0, :, cols(k)], wide.at[k], w_sem.at[k])

    def remote(src, dst, s, r, to):
        return pltpu.make_async_remote_copy(
            src_ref=src, dst_ref=dst, send_sem=s, recv_sem=r, device_id=to, device_id_type=MESH
        )

    def meas_copy(d, slot):
        return remote(meas_send.at[d], meas_recv.at[slot], ms_s.at[d], ms_r.at[slot], {"slab": d})

    def half_copy(k):
        return remote(half_send.at[k], half_recv.at[k], f_s.at[k], f_r.at[k], {"rep": other})

    def code_copy(k, d, slot):
        return remote(code_send.at[k, d], code_recv.at[k, slot], q_s.at[k, d], q_r.at[k, slot], {"slab": d})

    def res_copy(k, d, slot):
        src = gather.at[k, 0, me]
        return remote(src, gather.at[k, 0, slot], r_s.at[k, d], r_r.at[k, slot], {"slab": d})

    def pass_copy(k, s):
        return remote(gather.at[k, 0, s], gather.at[k, 1, s], p_s.at[k, s], p_r.at[k, s], {"rep": other})

    def x_copy(to, slot):
        return remote(x_send, x_recv.at[slot], x_s.at[to], x_r.at[slot], {"ang": to})

    def near(fn):
        def one(i):
            d = me + (span - i // 2) * (1 - 2 * (i % 2))

            @pl.when((d >= 0) & (d < slabs))
            def _():
                fn(d)

        each(2 * span, one)

    def others(count, mine, fn):
        each(count - 1, lambda i: fn(lax.rem(mine + i + 1, count)))

    small = [
        pltpu.make_async_copy(src, dst, in_sem.at[i])
        for i, (src, dst) in enumerate(
            ((bands_in, bands), (counts_in, counts), (tiles_in, tiles), (measured_in, measured), (volume_in, volume))
        )
    ]
    for copy in small:
        copy.start()
    for k in range(chunks):
        load(k).start()

    if angles < ROWS:
        meas_send[...] = jnp.zeros_like(meas_send)
        half_own[...] = jnp.zeros_like(half_own)
        half_send[...] = jnp.zeros_like(half_send)
    rows_t[...] = jnp.zeros_like(rows_t)
    gather[...] = jnp.zeros_like(gather)

    barrier = pltpu.get_barrier_semaphore()
    others(slabs, me, lambda d: pl.semaphore_signal(barrier, inc=1, device_id={"slab": d}, device_id_type=MESH))
    others(angs, ang, lambda d: pl.semaphore_signal(barrier, inc=1, device_id={"ang": d}, device_id_type=MESH))
    pl.semaphore_signal(barrier, inc=1, device_id={"rep": other}, device_id_type=MESH)

    for copy in small:
        copy.wait()

    def fill(d):
        for a in range(angles):
            meas_send[d, a : a + 1, LANES : LANES + strip] = measured[a, pl.ds(d * 2 + rep, 1), :]
            first = bands[0, 0, a]
            count = counts[0, a]
            listed = jnp.where((d >= first) & (d < first + count), F32(1), F32(0))
            slot = jnp.clip(d - first, 0, tiles.shape[2] - 1)
            rows_t[0, d, a : a + 1, 0:zs] = tiles[a, 0, slot, pl.ds(rep, 1), :] * listed
            rows_t[1, d, a : a + 1, 0:zs] = tiles[a, 0, slot, pl.ds(other, 1), :] * listed

    each(slabs, fill)

    lane = lax.broadcasted_iota(jnp.int32, (ROWS, LANES), 1)
    row = lax.broadcasted_iota(jnp.int32, (ROWS, LANES), 0)
    same = (lane // zs) == row

    def blocks(d):
        for r in range(2):
            y = rows_t[r, d]
            weight = jnp.sum(y, axis=1, keepdims=True)
            if r == 0:
                meas_send[d, :, 0:LANES] = jnp.broadcast_to(weight, (ROWS, LANES))
            width = zs
            while width < nz:
                y = y + pltpu.roll(y, width, 1)
                width *= 2
            y = jnp.where(same, y, 0.0)[:, :nz]
            at = block(r * slabs + d)
            bd_raw[at, :] = y
            bd_mean[at, :] = y * (mean_scale / jnp.maximum(weight, 1e-30))

    each(slabs, blocks)
    pl.semaphore_wait(barrier, slabs + angs - 1)
    others(slabs, me, lambda d: meas_copy(d, me).start())

    tw[...] = lax.dot_general(
        bd_raw[...], jnp.ones((2 * nrow, LANES), F32), (((0,), (0,)), ((), ())),
        precision=EXACT, preferred_element_type=F32,
    )
    acc[...] = jnp.zeros_like(acc)
    left = jnp.concatenate([volume[...], jnp.ones_like(volume)], axis=0).astype(BF16)

    def project(k):
        load(k).wait()
        for a in range(angles):
            if a == angles // 2 and k > 0:
                scatter(k - 1)
            got = jnp.dot(left, wide[k, a], preferred_element_type=F32)
            proj[a * zs : (a + 1) * zs, :] = got[0:zs]
            half_own[k, nrow + a : nrow + a + 1, :] = got[zs : zs + 1]
            half_send[k, nrow + a : nrow + a + 1, :] = got[zs : zs + 1]
        mix = jnp.dot(bd_mean[...], proj[...], precision=EXACT, preferred_element_type=F32)
        half_own[k, 0:nrow, :] = mix[0:nrow]
        half_send[k, 0:nrow, :] = mix[nrow:]
        half_copy(k).start()

    def scatter(k):
        half_copy(k).wait_recv()
        ones = half_own[k, nrow:, :] + half_recv[k, nrow:, :]
        ones_code = jnp.round(ones * ones_scale - HALF_CODE)

        def send(d):
            mean = half_own[k, block(d), :] + half_recv[k, block(d), :]
            code = jnp.concatenate([jnp.round(mean - HALF_CODE), ones_code], axis=0)
            code_send[k, d] = code.astype(jnp.int32).astype(jnp.int16)
            code_copy(k, d, me).start()

        near(send)

    def wide_weight(s):
        return jnp.concatenate([meas_recv[s, :, 0:LANES]] * (cw // LANES), axis=1)

    def own_weight():
        return jnp.concatenate([meas_send[me, :, 0:LANES]] * (cw // LANES), axis=1)

    def solve(k):
        if k == 0:
            others(slabs, me, lambda s: meas_copy(s, s).wait_recv())
            meas_recv[me] = meas_send[me]
        weight = own_weight()
        res_wide[0:ROWS, :] = weight * (half_own[k, block(me), :] + half_recv[k, block(me), :])
        res_wide[ROWS:, :] = weight * ((half_own[k, nrow:, :] + half_recv[k, nrow:, :]) * ones_scale)

        def add(s):
            code_copy(k, s, s).wait_recv()
            code = code_recv[k, s].astype(jnp.int32).astype(F32) + HALF_CODE
            weight = wide_weight(s)
            res_wide[0:ROWS, :] += weight * code[0:ROWS]
            res_wide[ROWS:, :] += weight * code[ROWS:]

        near(add)
        if strip <= cw:
            each_k = cw // strip
            row_meas = jnp.concatenate(
                [meas_recv[k * each_k + j, :, LANES : LANES + strip] for j in range(each_k)], axis=1
            )
        else:
            start = (k * cw) % strip
            row_meas = meas_recv[(k * cw) // strip, :, LANES + start : LANES + start + cw]
        res = (row_meas - res_wide[0:ROWS, :] * (1.0 / mean_scale)) / (res_wide[ROWS:, :] * (1.0 / ones_scale))
        if angles < ROWS:
            res = jnp.where(lax.broadcasted_iota(jnp.int32, res.shape, 0) < angles, res, 0.0)
        residual[:, cols(k)] = res[0:angles]
        gather[k, 0, me] = jnp.concatenate([res[:, : cw // 2], res[:, cw // 2 :]], axis=0).astype(BF16)
        near(lambda d: res_copy(k, d, me).start())
        pass_copy(k, me).start()

    def relay(k):
        def one(s):
            res_copy(k, s, s).wait_recv()
            pass_copy(k, s).start()

        near(one)

    def back(k):
        near(lambda s: pass_copy(k, s).wait_recv())
        pass_copy(k, me).wait_recv()
        for r in range(2):

            def spread(d):
                got = gather[k, r, d].astype(F32)
                at = block(r * slabs + d)
                res_all[at, : cw // 2] = got[0:ROWS]
                res_all[at, cw // 2 :] = got[ROWS:]

            each(slabs, spread)
        rows_back = lax.dot_general(
            bd_raw[...], res_all[...], (((0,), (0,)), ((), ())), precision=EXACT, preferred_element_type=F32
        )
        update = acc[0:zs, :]
        sums = acc[zs:, :]
        ones = jnp.ones((zs, cw), F32)
        for a in range(angles):
            lhs = jnp.concatenate([rows_back[a * zs : (a + 1) * zs], ones], axis=0).astype(BF16)
            got = lax.dot_general(lhs, wide[k, a], (((1,), (1,)), ((), ())), preferred_element_type=F32)
            update = update + got[0:zs]
            weight = jnp.concatenate([tw[a * zs : (a + 1) * zs, :]] * (xy // LANES), axis=1)
            sums = sums + weight * got[zs:]
        acc[0:zs, :] = update
        acc[zs:, :] = sums

    for k in range(chunks):
        project(k)
    scatter(chunks - 1)
    for k in range(chunks):
        solve(k)
    for k in range(chunks):
        relay(k)
        back(k)

    x_send[...] = acc[...]
    others(angs, ang, lambda to: x_copy(to, ang).start())
    others(angs, ang, lambda s: x_copy(s, s).wait_recv())
    x_recv[ang] = x_send[...]
    total = x_recv[0]
    for i in range(1, angs):
        total = total + x_recv[i]
    new_volume[...] = volume[...] + total[0:zs] / total[zs:]

    others(slabs, me, lambda d: meas_copy(d, me).wait_send())
    others(angs, ang, lambda to: x_copy(to, ang).wait_send())
    for k in range(chunks):
        half_copy(k).wait_send()
        pass_copy(k, me).wait_send()

        def done(d):
            code_copy(k, d, me).wait_send()
            res_copy(k, d, me).wait_send()
            pass_copy(k, d).wait_send()

        near(done)


def body(mesh, volume, measured, in_plane, pair_bands, pair_counts, pair_weight_tiles):
    slabs, angs = mesh.shape["slab"], mesh.shape["ang"]
    angles, _, xy, width = in_plane.shape
    zs = volume.shape[0]
    span = (pair_weight_tiles.shape[2] - 1) // 2
    chunks = CHUNKS
    cw = width // chunks
    strip = measured.shape[2]
    bands, counts = pair_bands.transpose(2, 1, 0), pair_counts.T
    cfg = (slabs, angs, span, angles, zs, cw, chunks, strip)
    nrow, nz = slabs * ROWS, angles * zs
    dma = pltpu.SemaphoreType.DMA
    vmem = pl.BlockSpec(memory_space=pltpu.VMEM)
    hbm = pl.BlockSpec(memory_space=pltpu.HBM)
    new_volume, residual = pl.pallas_call(
        functools.partial(kernel, cfg),
        out_shape=(pltpu.VMEM((zs, xy), F32), pltpu.VMEM((angles, width), F32)),
        in_specs=[hbm] * 6,
        out_specs=(vmem, vmem),
        scratch_shapes=[
            pltpu.VMEM(volume.shape, F32),
            pltpu.VMEM(measured.shape, F32),
            pltpu.SMEM(bands.shape, jnp.int32),
            pltpu.SMEM(counts.shape, jnp.int32),
            pltpu.VMEM(pair_weight_tiles.shape, F32),
            pltpu.VMEM((chunks, angles, xy, cw), BF16),
            pltpu.VMEM((2, slabs, ROWS, LANES), F32),
            pltpu.VMEM((2 * nrow, nz), F32),
            pltpu.VMEM((2 * nrow, nz), F32),
            pltpu.VMEM((nz, LANES), F32),
            pltpu.VMEM((nz, cw), F32),
            pltpu.VMEM((slabs, ROWS, LANES + strip), F32),
            pltpu.VMEM((slabs, ROWS, LANES + strip), F32),
            pltpu.VMEM((chunks, nrow + ROWS, cw), F32),
            pltpu.VMEM((chunks, nrow + ROWS, cw), F32),
            pltpu.VMEM((chunks, nrow + ROWS, cw), F32),
            pltpu.VMEM((chunks, slabs, 2 * ROWS, cw), jnp.int16),
            pltpu.VMEM((chunks, slabs, 2 * ROWS, cw), jnp.int16),
            pltpu.VMEM((chunks, 2, slabs, 2 * ROWS, cw // 2), BF16),
            pltpu.VMEM((2 * nrow, cw), F32),
            pltpu.VMEM((2 * ROWS, cw), F32),
            pltpu.VMEM((2 * zs, xy), F32),
            pltpu.VMEM((2 * zs, xy), F32),
            pltpu.VMEM((angs, 2 * zs, xy), F32),
            dma((5,)), dma((chunks,)),
            dma((slabs,)), dma((slabs,)),
            dma((chunks,)), dma((chunks,)),
            dma((chunks, slabs)), dma((chunks, slabs)),
            dma((chunks, slabs)), dma((chunks, slabs)),
            dma((chunks, slabs)), dma((chunks, slabs)),
            dma((angs,)), dma((angs,)),
        ],
        compiler_params=pltpu.CompilerParams(
            collective_id=0, has_side_effects=True, vmem_limit_bytes=60 * 1024 * 1024
        ),
        cost_estimate=pl.CostEstimate(
            flops=8 * angles * zs * xy * width, bytes_accessed=2 * angles * xy * width, transcendentals=0
        ),
    )(volume, measured, in_plane, bands, counts, pair_weight_tiles)
    return new_volume, residual.reshape(angles, 1, width)


def solution(mesh):
    return jax.shard_map(
        functools.partial(body, mesh),
        mesh=mesh,
        in_specs=(
            P(("grp", "slab"), "rep"),
            P(("grp", "ang"), None, "slab"),
            P("ang", "slab", "rep", None),
            P("ang", "slab", None),
            P("ang", "slab"),
            P("ang", "slab", None, None, None),
        ),
        out_specs=(P(("grp", "slab"), "rep"), P(("grp", "ang"), ("slab", "rep"), None)),
        check_vma=False,
    )
```

```python
import functools

import jax
import jax.numpy as jnp
from jax import lax
from jax.experimental import pallas as pl
from jax.experimental.pallas import tpu as pltpu
from jax.sharding import PartitionSpec as P

MESH = pl.DeviceIdType.MESH
F32 = jnp.float32
BF16 = jnp.bfloat16
EXACT = lax.Precision.HIGHEST
LANES = 128
ROWS = 8
WEIGHT_MAX = 0.0099487305
VOLUME_MAX = 2.0
HALF_CODE = 32500.0
CHUNKS = 2


def each(count, fn):
    if count <= 8:
        for i in range(count):
            fn(i)
    else:
        pl.loop(0, count)(fn)


def kernel(
    cfg,
    volume_in, measured_in, in_plane, bands_in, counts_in, tiles_in,
    new_volume, residual,
    volume, measured, bands, counts, tiles,
    wide, rows_t, bd_raw, bd_mean, tw, proj,
    meas_send, meas_recv, half_own, half_send, half_recv,
    code_send, code_recv, gather, res_all, res_wide, acc, x_send, x_recv,
    in_sem, w_sem, ms_s, ms_r, f_s, f_r, q_s, q_r, r_s, r_r, p_s, p_r, x_s, x_r,
):
    slabs, angs, span, angles, zs, cw, chunks, strip = cfg
    me = lax.axis_index("slab")
    rep = lax.axis_index("rep")
    ang = lax.axis_index("ang")
    other = 1 - rep
    nrow = slabs * ROWS
    nz = angles * zs
    xy = volume.shape[1]
    xy_all = 2 * xy
    mean_scale = 2 * HALF_CODE / (xy_all * VOLUME_MAX * WEIGHT_MAX * 1.001)
    ones_scale = 2 * HALF_CODE / (xy_all * WEIGHT_MAX * 1.001)

    def cols(k):
        return pl.ds(k * cw, cw)

    def block(d):
        return pl.ds(pl.multiple_of(d * ROWS, ROWS), ROWS)

    def load(k):
        return pltpu.make_async_copy(in_plane.at[:, 0, :, cols(k)], wide.at[k], w_sem.at[k])

    def remote(src, dst, s, r, to):
        return pltpu.make_async_remote_copy(
            src_ref=src, dst_ref=dst, send_sem=s, recv_sem=r, device_id=to, device_id_type=MESH
        )

    def meas_copy(d, slot):
        return remote(meas_send.at[d], meas_recv.at[slot], ms_s.at[d], ms_r.at[slot], {"slab": d})

    def half_copy(k):
        return remote(half_send.at[k], half_recv.at[k], f_s.at[k], f_r.at[k], {"rep": other})

    def code_copy(k, d, slot):
        return remote(code_send.at[k, d], code_recv.at[k, slot], q_s.at[k, d], q_r.at[k, slot], {"slab": d})

    def res_copy(k, d, slot):
        src = gather.at[k, 0, me]
        return remote(src, gather.at[k, 0, slot], r_s.at[k, d], r_r.at[k, slot], {"slab": d})

    def pass_copy(k, s):
        return remote(gather.at[k, 0, s], gather.at[k, 1, s], p_s.at[k, s], p_r.at[k, s], {"rep": other})

    def x_copy(to, slot):
        return remote(x_send, x_recv.at[slot], x_s.at[to], x_r.at[slot], {"ang": to})

    def near(fn, far=False):
        def one(i):
            d = me + (span - i // 2 if far else 1 + i // 2) * (1 - 2 * (i % 2))

            @pl.when((d >= 0) & (d < slabs))
            def _():
                fn(d)

        each(2 * span, one)

    def others(count, mine, fn):
        each(count - 1, lambda i: fn(lax.rem(mine + i + 1, count)))

    small = [
        pltpu.make_async_copy(src, dst, in_sem.at[i])
        for i, (src, dst) in enumerate(
            ((bands_in, bands), (counts_in, counts), (tiles_in, tiles), (measured_in, measured), (volume_in, volume))
        )
    ]
    for copy in small:
        copy.start()
    for k in range(chunks):
        load(k).start()

    if angles < ROWS:
        meas_send[...] = jnp.zeros_like(meas_send)
        half_own[...] = jnp.zeros_like(half_own)
        half_send[...] = jnp.zeros_like(half_send)
    rows_t[...] = jnp.zeros_like(rows_t)
    gather[...] = jnp.zeros_like(gather)

    barrier = pltpu.get_barrier_semaphore()
    others(slabs, me, lambda d: pl.semaphore_signal(barrier, inc=1, device_id={"slab": d}, device_id_type=MESH))
    others(angs, ang, lambda d: pl.semaphore_signal(barrier, inc=1, device_id={"ang": d}, device_id_type=MESH))
    pl.semaphore_signal(barrier, inc=1, device_id={"rep": other}, device_id_type=MESH)

    for copy in small:
        copy.wait()

    def fill(d):
        for a in range(angles):
            meas_send[d, a : a + 1, LANES : LANES + strip] = measured[a, pl.ds(d * 2 + rep, 1), :]
            first = bands[0, 0, a]
            count = counts[0, a]
            listed = jnp.where((d >= first) & (d < first + count), F32(1), F32(0))
            slot = jnp.clip(d - first, 0, tiles.shape[2] - 1)
            rows_t[0, d, a : a + 1, 0:zs] = tiles[a, 0, slot, pl.ds(rep, 1), :] * listed
            rows_t[1, d, a : a + 1, 0:zs] = tiles[a, 0, slot, pl.ds(other, 1), :] * listed

    each(slabs, fill)

    lane = lax.broadcasted_iota(jnp.int32, (ROWS, LANES), 1)
    row = lax.broadcasted_iota(jnp.int32, (ROWS, LANES), 0)
    same = (lane // zs) == row

    def blocks(d):
        for r in range(2):
            y = rows_t[r, d]
            weight = jnp.sum(y, axis=1, keepdims=True)
            if r == 0:
                meas_send[d, :, 0:LANES] = jnp.broadcast_to(weight, (ROWS, LANES))
            width = zs
            while width < nz:
                y = y + pltpu.roll(y, width, 1)
                width *= 2
            y = jnp.where(same, y, 0.0)[:, :nz]
            at = block(r * slabs + d)
            bd_raw[at, :] = y
            bd_mean[at, :] = y * (mean_scale / jnp.maximum(weight, 1e-30))

    each(slabs, blocks)
    pl.semaphore_wait(barrier, slabs + angs - 1)
    others(slabs, me, lambda d: meas_copy(d, me).start())

    tw[...] = lax.dot_general(
        bd_raw[...], jnp.ones((2 * nrow, LANES), F32), (((0,), (0,)), ((), ())),
        precision=EXACT, preferred_element_type=F32,
    )
    acc[...] = jnp.zeros_like(acc)
    left = jnp.concatenate([volume[...], jnp.ones_like(volume)], axis=0).astype(BF16)

    def project(k):
        load(k).wait()
        for a in range(angles):
            if a == angles // 2 and k > 0:
                scatter(k - 1)
            got = jnp.dot(left, wide[k, a], preferred_element_type=F32)
            proj[a * zs : (a + 1) * zs, :] = got[0:zs]
            half_own[k, nrow + a : nrow + a + 1, :] = got[zs : zs + 1]
            half_send[k, nrow + a : nrow + a + 1, :] = got[zs : zs + 1]
        mix = jnp.dot(bd_mean[...], proj[...], precision=EXACT, preferred_element_type=F32)
        half_own[k, 0:nrow, :] = mix[0:nrow]
        half_send[k, 0:nrow, :] = mix[nrow:]
        half_copy(k).start()

    def scatter(k):
        half_copy(k).wait_recv()
        ones = half_own[k, nrow:, :] + half_recv[k, nrow:, :]
        ones_code = jnp.round(ones * ones_scale - HALF_CODE)

        def send(d):
            mean = half_own[k, block(d), :] + half_recv[k, block(d), :]
            code = jnp.concatenate([jnp.round(mean - HALF_CODE), ones_code], axis=0)
            code_send[k, d] = code.astype(jnp.int32).astype(jnp.int16)
            code_copy(k, d, me).start()

        near(send, True)

    def wide_weight(s):
        return jnp.concatenate([meas_recv[s, :, 0:LANES]] * (cw // LANES), axis=1)

    def own_weight():
        return jnp.concatenate([meas_send[me, :, 0:LANES]] * (cw // LANES), axis=1)

    def solve(k):
        if k == 0:
            others(slabs, me, lambda s: meas_copy(s, s).wait_recv())
            meas_recv[me] = meas_send[me]
        weight = own_weight()
        res_wide[0:ROWS, :] = weight * (half_own[k, block(me), :] + half_recv[k, block(me), :])
        res_wide[ROWS:, :] = weight * ((half_own[k, nrow:, :] + half_recv[k, nrow:, :]) * ones_scale)

        def add(s):
            code_copy(k, s, s).wait_recv()
            code = code_recv[k, s].astype(jnp.int32).astype(F32) + HALF_CODE
            weight = wide_weight(s)
            res_wide[0:ROWS, :] += weight * code[0:ROWS]
            res_wide[ROWS:, :] += weight * code[ROWS:]

        near(add)
        if strip <= cw:
            each_k = cw // strip
            row_meas = jnp.concatenate(
                [meas_recv[k * each_k + j, :, LANES : LANES + strip] for j in range(each_k)], axis=1
            )
        else:
            start = (k * cw) % strip
            row_meas = meas_recv[(k * cw) // strip, :, LANES + start : LANES + start + cw]
        res = (row_meas - res_wide[0:ROWS, :] * (1.0 / mean_scale)) / (res_wide[ROWS:, :] * (1.0 / ones_scale))
        if angles < ROWS:
            res = jnp.where(lax.broadcasted_iota(jnp.int32, res.shape, 0) < angles, res, 0.0)
        residual[:, cols(k)] = res[0:angles]
        gather[k, 0, me] = jnp.concatenate([res[:, : cw // 2], res[:, cw // 2 :]], axis=0).astype(BF16)
        near(lambda d: res_copy(k, d, me).start(), True)
        pass_copy(k, me).start()

    def relay(k):
        def one(s):
            res_copy(k, s, s).wait_recv()
            pass_copy(k, s).start()

        near(one)

    def back(k):
        near(lambda s: pass_copy(k, s).wait_recv())
        pass_copy(k, me).wait_recv()
        for r in range(2):

            def spread(d):
                got = gather[k, r, d].astype(F32)
                at = block(r * slabs + d)
                res_all[at, : cw // 2] = got[0:ROWS]
                res_all[at, cw // 2 :] = got[ROWS:]

            each(slabs, spread)
        rows_back = lax.dot_general(
            bd_raw[...], res_all[...], (((0,), (0,)), ((), ())), precision=EXACT, preferred_element_type=F32
        )
        update = acc[0:zs, :]
        sums = acc[zs:, :]
        ones = jnp.ones((zs, cw), F32)
        for a in range(angles):
            lhs = jnp.concatenate([rows_back[a * zs : (a + 1) * zs], ones], axis=0).astype(BF16)
            got = lax.dot_general(lhs, wide[k, a], (((1,), (1,)), ((), ())), preferred_element_type=F32)
            update = update + got[0:zs]
            weight = jnp.concatenate([tw[a * zs : (a + 1) * zs, :]] * (xy // LANES), axis=1)
            sums = sums + weight * got[zs:]
        acc[0:zs, :] = update
        acc[zs:, :] = sums

    for k in range(chunks):
        project(k)
    scatter(chunks - 1)
    for k in range(chunks):
        solve(k)
    for k in range(chunks):
        relay(k)
        back(k)

    x_send[...] = acc[...]
    others(angs, ang, lambda to: x_copy(to, ang).start())
    others(angs, ang, lambda s: x_copy(s, s).wait_recv())
    x_recv[ang] = x_send[...]
    total = x_recv[0]
    for i in range(1, angs):
        total = total + x_recv[i]
    new_volume[...] = volume[...] + total[0:zs] / total[zs:]

    others(slabs, me, lambda d: meas_copy(d, me).wait_send())
    others(angs, ang, lambda to: x_copy(to, ang).wait_send())
    for k in range(chunks):
        half_copy(k).wait_send()
        pass_copy(k, me).wait_send()

        def done(d):
            code_copy(k, d, me).wait_send()
            res_copy(k, d, me).wait_send()
            pass_copy(k, d).wait_send()

        near(done)


def body(mesh, volume, measured, in_plane, pair_bands, pair_counts, pair_weight_tiles):
    slabs, angs = mesh.shape["slab"], mesh.shape["ang"]
    angles, _, xy, width = in_plane.shape
    zs = volume.shape[0]
    span = (pair_weight_tiles.shape[2] - 1) // 2
    chunks = CHUNKS
    cw = width // chunks
    strip = measured.shape[2]
    bands, counts = pair_bands.transpose(2, 1, 0), pair_counts.T
    cfg = (slabs, angs, span, angles, zs, cw, chunks, strip)
    nrow, nz = slabs * ROWS, angles * zs
    dma = pltpu.SemaphoreType.DMA
    vmem = pl.BlockSpec(memory_space=pltpu.VMEM)
    hbm = pl.BlockSpec(memory_space=pltpu.HBM)
    new_volume, residual = pl.pallas_call(
        functools.partial(kernel, cfg),
        out_shape=(pltpu.VMEM((zs, xy), F32), pltpu.VMEM((angles, width), F32)),
        in_specs=[hbm] * 6,
        out_specs=(vmem, vmem),
        scratch_shapes=[
            pltpu.VMEM(volume.shape, F32),
            pltpu.VMEM(measured.shape, F32),
            pltpu.SMEM(bands.shape, jnp.int32),
            pltpu.SMEM(counts.shape, jnp.int32),
            pltpu.VMEM(pair_weight_tiles.shape, F32),
            pltpu.VMEM((chunks, angles, xy, cw), BF16),
            pltpu.VMEM((2, slabs, ROWS, LANES), F32),
            pltpu.VMEM((2 * nrow, nz), F32),
            pltpu.VMEM((2 * nrow, nz), F32),
            pltpu.VMEM((nz, LANES), F32),
            pltpu.VMEM((nz, cw), F32),
            pltpu.VMEM((slabs, ROWS, LANES + strip), F32),
            pltpu.VMEM((slabs, ROWS, LANES + strip), F32),
            pltpu.VMEM((chunks, nrow + ROWS, cw), F32),
            pltpu.VMEM((chunks, nrow + ROWS, cw), F32),
            pltpu.VMEM((chunks, nrow + ROWS, cw), F32),
            pltpu.VMEM((chunks, slabs, 2 * ROWS, cw), jnp.int16),
            pltpu.VMEM((chunks, slabs, 2 * ROWS, cw), jnp.int16),
            pltpu.VMEM((chunks, 2, slabs, 2 * ROWS, cw // 2), BF16),
            pltpu.VMEM((2 * nrow, cw), F32),
            pltpu.VMEM((2 * ROWS, cw), F32),
            pltpu.VMEM((2 * zs, xy), F32),
            pltpu.VMEM((2 * zs, xy), F32),
            pltpu.VMEM((angs, 2 * zs, xy), F32),
            dma((5,)), dma((chunks,)),
            dma((slabs,)), dma((slabs,)),
            dma((chunks,)), dma((chunks,)),
            dma((chunks, slabs)), dma((chunks, slabs)),
            dma((chunks, slabs)), dma((chunks, slabs)),
            dma((chunks, slabs)), dma((chunks, slabs)),
            dma((angs,)), dma((angs,)),
        ],
        compiler_params=pltpu.CompilerParams(
            collective_id=0, has_side_effects=True, vmem_limit_bytes=60 * 1024 * 1024
        ),
        cost_estimate=pl.CostEstimate(
            flops=8 * angles * zs * xy * width, bytes_accessed=2 * angles * xy * width, transcendentals=0
        ),
    )(volume, measured, in_plane, bands, counts, pair_weight_tiles)
    return new_volume, residual.reshape(angles, 1, width)


def solution(mesh):
    return jax.shard_map(
        functools.partial(body, mesh),
        mesh=mesh,
        in_specs=(
            P(("grp", "slab"), "rep"),
            P(("grp", "ang"), None, "slab"),
            P("ang", "slab", "rep", None),
            P("ang", "slab", None),
            P("ang", "slab"),
            P("ang", "slab", None, None, None),
        ),
        out_specs=(P(("grp", "slab"), "rep"), P(("grp", "ang"), ("slab", "rep"), None)),
        check_vma=False,
    )
```
